32 devices in a mesh: groups: 2 (over y), dp: 4 (over z), tensor: 4 (over x, core).
Axes of the slice: x: 2, y: 2, z: 4, core: 2. Of those that a mesh axis runs over, the one named last changes fastest.
Arguments:
- residual: bfloat16 [8192, 8192], P(('groups', 'dp'), 'tensor'), parts along dimension 0, may hold values from -128 to 128, as said below
- norm_gain: float32 [8192], P('tensor'), may hold values from 0.5 to 1.5
- key_weight: bfloat16 [8192, 512], P('tensor'), may hold values from -0.0625 to 0.0625
- value_weight: bfloat16 [8192, 512], P('tensor'), may hold values from -0.0625 to 0.0625
- key_grad: bfloat16 [8192, 512], P(('groups', 'dp', 'tensor')), parts along dimension 0, may hold values from -6 to 6
- value_grad: bfloat16 [8192, 512], P(('groups', 'dp', 'tensor')), parts along dimension 0, may hold values from -6 to 6
- key_left: bfloat16 [8192, 64], P('tensor'), may hold values from -0.0625 to 0.0625
- value_left: bfloat16 [8192, 64], P('tensor'), may hold values from -0.0625 to 0.0625
- key_right: bfloat16 [512, 64], replicated, may hold values from -0.25 to 0.25
- value_right: bfloat16 [512, 64], replicated, may hold values from -0.25 to 0.25
- queries: bfloat16 [64, 8192], P(('dp', 'tensor')), may hold values from -1.5 to 1.5
- doc_lengths: int32 [8], P(('groups', 'dp')), parts along dimension 0, may hold values from 128 to 1024
Outputs:
- key_out: bfloat16 [8192, 512], P(('groups', 'dp', 'tensor')), parts along dimension 0
- value_out: bfloat16 [8192, 512], P(('groups', 'dp', 'tensor')), parts along dimension 0
- hidden_grad: bfloat16 [8192, 8192], P(('groups', 'dp'), 'tensor'), parts along dimension 0
- scores: float32 [8, 64], P('groups', ('dp', 'tensor')), parts along dimension 0
The draws below stay inside these ranges and needn't reach their ends.
There are 2 independent parts, one for each index of `groups`. The reference program is written for one: setup_inputs(seed, part) draws one part's arguments, and reference() takes and returns one part's arrays. A program takes and returns all parts, laid end to end along the dimension named above; an argument that names none is the same for every part. Nothing has to cross between parts.
Inputs may be any that keep to these rules, and one draw needn't show every extreme that they name: `residual`: each entry is a token's feature; padding slots hold numbers too. `doc_lengths`: the number of leading slots of each document that hold tokens; the rest are padding.
All inputs are finite; a program needn't handle non-finite values.
Results may differ from the reference program's by a relative error of at most 0.019.
Values may be sent and summed in bfloat16 or wider, within the bound.
A program may use at most 64 MiB of HBM per device.

```python
import math
import jax
import jax.numpy as jnp
from jax import lax

D = 8192
KVW = 512
RANK = 64
MATS = 2
TOK_DEV = 1024
DOCS = 4
TOKENS = 4096
QUERIES = 64
N_DP = 4
N_TENSOR = 4


def draw_residual(key, part):
    key = jax.random.fold_in(key, 11)
    first, second, third = jax.random.split(key, 3)
    column = jnp.arange(D, dtype=jnp.float32)[None, :] / D
    base = jnp.clip(jax.random.normal(first, (TOKENS, D), jnp.float32), -4.0, 4.0)
    upper = math.log(10.0)
    rise = jnp.exp(0.5 * math.log(3.0) * column)
    row_scale = jnp.exp(jax.random.uniform(second, (TOKENS, 1), jnp.float32, 0.0, upper))
    col_scale = rise * jnp.exp(jax.random.uniform(third, (1, D), jnp.float32, math.log(0.8), math.log(1.25)))
    return (base * row_scale * col_scale).astype(jnp.bfloat16)


def touch_ends(entries, stream_key, least, high):
    longest = entries.shape.index(max(entries.shape))
    spots = []
    for shift in (0, 1):
        where = [jax.random.randint(jax.random.fold_in(stream_key, axis), (), 0, length) for axis, length in enumerate(entries.shape)]
        where[longest] = (where[longest] + shift) % entries.shape[longest]
        spots.append(tuple(where))
    return entries.at[spots[0]].set(least).at[spots[1]].set(high)


def shard_levels(own_key, dims, cuts, least, high):
    loudness, own = 1.0, jax.random.fold_in(own_key, 6)
    for dim, shards_of in cuts:
        heights = jnp.exp(jax.random.uniform(jax.random.fold_in(own, dim), (shards_of,), jnp.float32, least / len(cuts), high / len(cuts)))
        loudness = loudness * jnp.repeat(heights, dims[dim] // shards_of).reshape([-1 if axis == dim else 1 for axis in range(len(dims))])
    return loudness


def centred(own_key, extent, deviation, limit, cuts=(), kind=jnp.bfloat16):
    drawn = deviation * jax.random.normal(own_key, extent, jnp.float32)
    if cuts:
        drawn = drawn * shard_levels(own_key, extent, cuts, -0.22, 0.18)
    return jnp.clip(drawn, -limit, limit).astype(kind)


def setup_inputs(seed: int = 0, part: int = 0) -> dict:
    key_of = jax.random.split(jax.random.key(seed), 13)
    part_splits = jax.random.split(jax.random.fold_in(key_of[12], part), 13)
    return {
        "residual": draw_residual(jax.random.fold_in(jax.random.fold_in(key_of[12], part), 71), part),
        "norm_gain": jnp.clip(1.0 + 0.1 * jax.random.normal(key_of[1], (D,), jnp.float32), 0.5, 1.5),
        "key_weight": centred(key_of[2], (D, KVW), D ** -0.5, 0.0625, ((0, 4),)),
        "value_weight": centred(key_of[3], (D, KVW), D ** -0.5, 0.0625, ((0, 4),)),
        "key_grad": centred(part_splits[4], (TOKENS, KVW), 1.0, 6.0, ((0, 16),)),
        "value_grad": centred(part_splits[5], (TOKENS, KVW), 1.0, 6.0, ((0, 16),)),
        "key_left": centred(key_of[6], (D, RANK), D ** -0.5, 0.0625, ((0, 4),)),
        "value_left": centred(key_of[7], (D, RANK), D ** -0.5, 0.0625, ((0, 4),)),
        "key_right": centred(key_of[8], (KVW, RANK), KVW ** -0.5, 0.25),
        "value_right": centred(key_of[9], (KVW, RANK), KVW ** -0.5, 0.25),
        "queries": centred(key_of[10], (QUERIES, MATS * RANK * RANK), 0.25, 1.5, ((0, 16),)),
        "doc_lengths": touch_ends(jax.random.randint(part_splits[11], (DOCS,), TOK_DEV // 8, TOK_DEV + 1), jax.random.fold_in(part_splits[11], 1), TOK_DEV // 8, TOK_DEV).astype(jnp.int32),
    }


def rounded_add(total, term):
    kept = lax.optimization_barrier(term.astype(jnp.bfloat16))
    return total + kept.astype(jnp.float32)

def gram_rows(first, masked, right):
    second = jnp.dot(masked, right, preferred_element_type=jnp.float32).reshape(N_DP, TOK_DEV, RANK)
    first = first.reshape(N_DP, TOK_DEV, RANK)
    product = jnp.einsum('dtr,dts->drs', first, second, precision=lax.Precision.HIGHEST) / TOK_DEV
    return product.reshape(N_DP, RANK * RANK)

def reference(residual, norm_gain, key_weight, value_weight, key_grad, value_grad, key_left, value_left, key_right, value_right, queries, doc_lengths):
    widened = residual.astype(jnp.float32)
    inverse = lax.rsqrt(lax.optimization_barrier(jnp.mean(widened * widened, axis=1, keepdims=True)) + 1e-05)
    normed = (widened * inverse * norm_gain).astype(jnp.bfloat16)
    block = D // N_TENSOR
    key_sum = jnp.zeros((TOKENS, KVW), jnp.float32)
    value_sum = jnp.zeros((TOKENS, KVW), jnp.float32)
    left_key = jnp.zeros((TOKENS, RANK), jnp.float32)
    left_value = jnp.zeros((TOKENS, RANK), jnp.float32)
    for index in range(N_TENSOR):
        lower = index * block
        upper = lower + block
        slab = normed[:, lower:upper]
        key_sum = rounded_add(key_sum, jnp.dot(slab, key_weight[lower:upper], preferred_element_type=jnp.float32))
        value_sum = rounded_add(value_sum, jnp.dot(slab, value_weight[lower:upper], preferred_element_type=jnp.float32))
        left_key = rounded_add(left_key, jnp.dot(slab, key_left[lower:upper], preferred_element_type=jnp.float32))
        left_value = rounded_add(left_value, jnp.dot(slab, value_left[lower:upper], preferred_element_type=jnp.float32))
    key_out = key_sum.astype(jnp.bfloat16)
    value_out = value_sum.astype(jnp.bfloat16)
    position = jnp.arange(TOKENS, dtype=jnp.int32)
    owner = position // TOK_DEV
    live = (position % TOK_DEV < doc_lengths[owner]).astype(jnp.bfloat16)[:, None]
    key_masked = key_grad * live
    value_masked = value_grad * live
    back = jnp.dot(key_masked, key_weight.T, preferred_element_type=jnp.float32)
    back = back + jnp.dot(value_masked, value_weight.T, preferred_element_type=jnp.float32)
    hidden_grad = back.astype(jnp.bfloat16)
    key_gram = gram_rows(left_key, key_masked, key_right)
    value_gram = gram_rows(left_value, value_masked, value_right)
    flat = jnp.concatenate([key_gram, value_gram], axis=1).astype(jnp.bfloat16)
    scores = jnp.dot(flat, queries.T, preferred_element_type=jnp.float32)
    return (key_out, value_out, hidden_grad, scores)
```

```python
import functools

import jax
import jax.numpy as jnp
from jax import lax
from jax.experimental import pallas as pl
from jax.experimental.pallas import tpu as pltpu
from jax.sharding import PartitionSpec as P

F32, BF16 = jnp.float32, jnp.bfloat16
LANES = 128


def kernel(
    parts,
    docs,
    residual,
    gain,
    key_weight,
    value_weight,
    key_grad,
    value_grad,
    key_left,
    value_left,
    key_right,
    value_right,
    queries,
    length,
    key_out,
    value_out,
    hidden_out,
    score_out,
    res_v,
    gain_v,
    kw_v,
    vw_v,
    kl_v,
    vl_v,
    left_w,
    kr_v,
    vr_v,
    got_k,
    got_v,
    mask_k,
    mask_v,
    partial,
    sib_in,
    x_out,
    x_in,
    left_t,
    squares,
    gram_rows,
    gram_in,
    flat_in,
    hid_v,
    load_sem,
    res_sem,
    own_sem,
    hid_sem,
    ag_sib_s,
    ag_sib_r,
    ag_x_s,
    ag_x_r,
    ag_f_s,
    ag_f_r,
    rs_sib_s,
    rs_sib_r,
    rs_x_s,
    rs_x_r,
    sq_s,
    sq_r,
    gr_s,
    gr_r,
    fl_s,
    fl_r,
):
    chips = parts // 2
    slots, features = res_v.shape
    rows = slots // parts
    columns = kw_v.shape[1]
    rank = kl_v.shape[1]
    me = lax.axis_index("tensor")
    doc = lax.axis_index("dp")
    chip, core = me // 2, lax.rem(me, 2)
    sibling = chip * 2 + 1 - core

    def send(src, dst, s_sem, r_sem, target):
        return pltpu.make_async_remote_copy(
            src_ref=src,
            dst_ref=dst,
            send_sem=s_sem,
            recv_sem=r_sem,
            device_id=target,
            device_id_type=pl.DeviceIdType.MESH,
        )

    def chip_at(step):
        return lax.rem(chip + step + chips, chips)

    def block_of(order):
        step = lax.rem(order // 2 + 1, chips)
        other = lax.rem(order, 2)
        return chip_at(step) * 2 + jnp.where(other == 0, 1 - core, core)

    loads = [
        pltpu.make_async_copy(src, dst, load_sem.at[i])
        for i, (src, dst) in enumerate(
            (
                (gain, gain_v),
                (key_weight, kw_v),
                (value_weight, vw_v),
                (key_left, kl_v),
                (value_left, vl_v),
                (key_right, kr_v),
                (value_right, vr_v),
            )
        )
    ]

    def res_copy(order):
        at = pl.ds(pl.multiple_of(block_of(order) * rows, rows), rows)
        return pltpu.make_async_copy(residual.at[at], res_v.at[at], res_sem.at[order])

    own_copies = [
        pltpu.make_async_copy(key_grad, got_k.at[me], own_sem.at[0]),
        pltpu.make_async_copy(value_grad, got_v.at[me], own_sem.at[1]),
    ]

    barrier = pltpu.get_barrier_semaphore()
    for step in range(1, parts):
        pl.semaphore_signal(
            barrier, inc=1, device_id={"tensor": lax.rem(me + step, parts)},
            device_id_type=pl.DeviceIdType.MESH,
        )

    def greet(step, carry):
        pl.semaphore_signal(
            barrier, inc=1, device_id={"dp": lax.rem(doc + step, docs)},
            device_id_type=pl.DeviceIdType.MESH,
        )
        return carry

    lax.fori_loop(1, docs, greet, 0)
    for copy in loads[:5]:
        copy.start()
    for order in range(parts):
        res_copy(order).start()
    for copy in loads[5:]:
        copy.start()
    for copy in own_copies:
        copy.start()
    pl.semaphore_wait(barrier, parts - 1 + docs - 1)

    grads = ((key_grad, got_k), (value_grad, got_v))
    ag_x = [
        [
            send(src, got.at[me], ag_x_s.at[step - 1, i], ag_x_r.at[step - 1, i],
                 {"tensor": chip_at(step) * 2 + core})
            for i, (src, got) in enumerate(grads)
        ]
        for step in range(1, chips)
    ]
    ag_sib = [
        send(src, got.at[me], ag_sib_s.at[i], ag_sib_r.at[i], {"tensor": sibling})
        for i, (src, got) in enumerate(grads)
    ]
    for pair in ag_x:
        for copy in pair:
            copy.start()
    for copy in ag_sib:
        copy.start()

    for copy in loads:
        copy.wait()
    left_w[:, :rank] = kl_v[...]
    left_w[:, rank:] = vl_v[...]

    def rs_sib(at):
        return send(partial.at[2 * at], sib_in.at[at], rs_sib_s.at[at], rs_sib_r.at[at],
                    {"tensor": sibling})

    def forward(order, carry):
        res_copy(order).wait()
        block = block_of(order)
        wide = res_v[pl.ds(pl.multiple_of(block * rows, rows), rows), :].astype(F32)
        scaled = (wide * gain_v[...]).astype(BF16)
        squared = wide * wide
        lane_sum = squared[:, :LANES]
        for i in range(1, features // LANES):
            lane_sum = lane_sum + squared[:, i * LANES : (i + 1) * LANES]
        squares[me, pl.ds(block, 1), :] = jnp.sum(lane_sum.T, axis=0, keepdims=True)
        partial[order, :, :columns] = jnp.dot(
            scaled, kw_v[...], preferred_element_type=F32
        ).astype(BF16)
        partial[order, :, columns:] = jnp.dot(
            scaled, vw_v[...], preferred_element_type=F32
        ).astype(BF16)
        left_t[block] = jnp.dot(scaled, left_w[...], preferred_element_type=F32).T

        @pl.when(lax.rem(order, 2) == 0)
        def _():
            rs_sib(order // 2).start()

        return carry

    lax.fori_loop(0, parts, forward, 0)

    sq = [
        send(squares.at[me], squares.at[me], sq_s.at[step - 1], sq_r.at[step - 1],
             {"tensor": lax.rem(me + step, parts)})
        for step in range(1, parts)
    ]
    for copy in sq:
        copy.start()

    rs_x = []
    for step in range(1, chips):
        at = step - 1
        rs_sib(at).wait_recv()
        x_out[at] = (
            partial[2 * at + 1].astype(F32) + sib_in[at].astype(F32)
        ).astype(BF16)
        rs_x.append(
            send(x_out.at[at], x_in.at[at], rs_x_s.at[at], rs_x_r.at[at],
                 {"tensor": chip_at(step) * 2 + core})
        )

    def inverse_of(block):
        total = squares[0, pl.ds(block, 1), :]
        for i in range(1, parts):
            total = total + squares[i, pl.ds(block, 1), :]
        return lax.rsqrt(total / (features * parts) + 1e-05)

    span = 2 * rows
    tile = min(features, 512)

    def mask_chip(at):
        for half in range(2):
            block = at * 2 + half
            place = block * rows + lax.broadcasted_iota(jnp.int32, (rows, columns), 0)
            live = (place < length[0]).astype(F32).astype(BF16)
            mask_k[half * rows : (half + 1) * rows, :] = got_k[block] * live
            mask_v[half * rows : (half + 1) * rows, :] = got_v[block] * live

    def gram_add(at, first):
        right_k = jnp.dot(mask_k[...], kr_v[...], preferred_element_type=F32)
        right_v = jnp.dot(mask_v[...], vr_v[...], preferred_element_type=F32)
        for half in range(2):
            block = at * 2 + half
            left = left_t[block] * inverse_of(block)
            for i, right in enumerate((right_k, right_v)):
                term = jnp.dot(
                    left[i * rank : (i + 1) * rank],
                    right[half * rows : (half + 1) * rows],
                    precision=lax.Precision.HIGHEST,
                    preferred_element_type=F32,
                )
                here = slice(i * rank, (i + 1) * rank)
                if first and half == 0:
                    gram_rows[here, :] = term
                else:
                    gram_rows[here, :] += term

    def hid_copy(at):
        to = pl.ds(pl.multiple_of(at * span, span), span)
        return pltpu.make_async_copy(hid_v.at[to], hidden_out.at[to], hid_sem.at[at])

    def back(at):
        to = pl.ds(pl.multiple_of(at * span, span), span)
        contract = (((1,), (1,)), ((), ()))

        def one(i, carry):
            here = pl.ds(pl.multiple_of(i * tile, tile), tile)
            total = lax.dot_general(
                mask_k[...], kw_v[here, :], contract, preferred_element_type=F32
            ) + lax.dot_general(
                mask_v[...], vw_v[here, :], contract, preferred_element_type=F32
            )
            hid_v[to, here] = total.astype(BF16)
            return carry

        lax.fori_loop(0, features // tile, one, 0)
        hid_copy(at).start()

    for copy in own_copies:
        copy.wait()
    for copy in ag_sib:
        copy.wait_recv()
    mask_chip(chip)
    back(chip)
    for copy in sq:
        copy.wait_recv()
    gram_add(chip, True)

    for pair in ag_x:
        for copy in pair:
            copy.wait_send()
    for copy in rs_x:
        copy.start()
    passed = []
    for step in range(1, chips):
        origin = chip_at(-step) * 2 + core
        for i, (_, got) in enumerate(grads):
            ag_x[step - 1][i].wait_recv()
            copy = send(got.at[origin], got.at[origin], ag_f_s.at[step - 1, i],
                        ag_f_r.at[step - 1, i], {"tensor": sibling})
            copy.start()
            passed.append(copy)

    for step in range(1, chips):
        at = chip_at(-step)
        for i in range(2):
            passed[2 * (step - 1) + i].wait_recv()
        mask_chip(at)
        gram_add(at, False)
        if step == chips - 1:
            half = gram_rows.shape[0] // 2
            gram_in[me] = jnp.concatenate(
                [gram_rows[pl.ds(0, half, stride=2), :], gram_rows[pl.ds(1, half, stride=2), :]],
                axis=1,
            )
            gr = [
                send(gram_in.at[me], gram_in.at[me], gr_s.at[to - 1], gr_r.at[to - 1],
                     {"tensor": lax.rem(me + to, parts)})
                for to in range(1, parts)
            ]
            for copy in gr:
                copy.start()
        back(at)

    for copy in gr:
        copy.wait_recv()
    gram = gram_in[0]
    for i in range(1, parts):
        gram = gram + gram_in[i]
    flat_in[doc] = (gram / slots).astype(BF16)

    def flat_copy(step):
        return send(flat_in.at[doc], flat_in.at[doc], fl_s.at[step - 1], fl_r.at[step - 1],
                    {"dp": lax.rem(doc + step, docs)})

    def flat_start(step, carry):
        flat_copy(step).start()
        return carry

    def flat_wait(step, carry):
        flat_copy(step).wait()
        return carry

    lax.fori_loop(1, docs, flat_start, 0)

    last = chips - 1
    rs_sib(last).wait_recv()
    own = partial[2 * last + 1].astype(F32) + sib_in[last].astype(F32)
    inverse = jnp.broadcast_to(inverse_of(me), (LANES, rows)).T

    lax.fori_loop(1, docs, flat_wait, 0)

    def score(i, carry):
        flat = flat_in[i].astype(F32)
        total = jnp.zeros((queries.shape[0], LANES), F32)
        for j in range(flat.shape[0]):
            total = total + queries[:, j * LANES : (j + 1) * LANES].astype(F32) * flat[j : j + 1]
        score_out[i] = total
        return carry

    lax.fori_loop(0, docs, score, 0)

    for copy in rs_x:
        copy.wait_recv()
    for i in range(chips - 1):
        own = own + x_in[i].astype(F32)
    for i in range(columns // LANES):
        here = slice(i * LANES, (i + 1) * LANES)
        there = slice(columns + i * LANES, columns + (i + 1) * LANES)
        key_out[:, here] = (own[:, here] * inverse).astype(BF16)
        value_out[:, here] = (own[:, there] * inverse).astype(BF16)

    for copy in ag_sib + passed + sq + gr + rs_x:
        copy.wait_send()
    for i in range(chips):
        rs_sib(i).wait_send()
        hid_copy(i).wait()


def body(
    residual,
    norm_gain,
    key_weight,
    value_weight,
    key_grad,
    value_grad,
    key_left,
    value_left,
    key_right,
    value_right,
    queries,
    doc_lengths,
):
    parts, docs = lax.axis_size("tensor"), lax.axis_size("dp")
    chips = parts // 2
    slots, features = residual.shape
    rows = slots // parts
    columns, rank = key_weight.shape[1], key_left.shape[1]
    hbm = pl.BlockSpec(memory_space=pl.ANY)
    vmem = pl.BlockSpec(memory_space=pltpu.VMEM)
    dma = pltpu.SemaphoreType.DMA
    flat_rows = 2 * rank * rank // LANES
    key_out, value_out, hidden_grad, shares = pl.pallas_call(
        functools.partial(kernel, parts, docs),
        out_shape=(
            jax.ShapeDtypeStruct((rows, columns), BF16),
            jax.ShapeDtypeStruct((rows, columns), BF16),
            jax.ShapeDtypeStruct((slots, features), BF16),
            jax.ShapeDtypeStruct((docs, queries.shape[0], LANES), F32),
        ),
        in_specs=[hbm] * 10 + [vmem, pl.BlockSpec(memory_space=pltpu.SMEM)],
        out_specs=(vmem, vmem, hbm, vmem),
        scratch_shapes=[
            pltpu.VMEM((slots, features), BF16),
            pltpu.VMEM((1, features), F32),
            pltpu.VMEM((features, columns), BF16),
            pltpu.VMEM((features, columns), BF16),
            pltpu.VMEM((features, rank), BF16),
            pltpu.VMEM((features, rank), BF16),
            pltpu.VMEM((features, 2 * rank), BF16),
            pltpu.VMEM((columns, rank), BF16),
            pltpu.VMEM((columns, rank), BF16),
            pltpu.VMEM((parts, rows, columns), BF16),
            pltpu.VMEM((parts, rows, columns), BF16),
            pltpu.VMEM((2 * rows, columns), BF16),
            pltpu.VMEM((2 * rows, columns), BF16),
            pltpu.VMEM((parts, rows, 2 * columns), BF16),
            pltpu.VMEM((chips, rows, 2 * columns), BF16),
            pltpu.VMEM((chips - 1, rows, 2 * columns), BF16),
            pltpu.VMEM((chips - 1, rows, 2 * columns), BF16),
            pltpu.VMEM((parts, 2 * rank, rows), F32),
            pltpu.VMEM((parts, parts, rows), F32),
            pltpu.VMEM((2 * rank, rank), F32),
            pltpu.VMEM((parts, flat_rows, LANES), F32),
            pltpu.VMEM((docs, flat_rows, LANES), BF16),
            pltpu.VMEM((slots, features), BF16),
            dma((7,)),
            dma((parts,)),
            dma((2,)),
            dma((chips,)),
            dma((2,)),
            dma((2,)),
            dma((chips - 1, 2)),
            dma((chips - 1, 2)),
            dma((chips - 1, 2)),
            dma((chips - 1, 2)),
            dma((chips,)),
            dma((chips,)),
            dma((chips - 1,)),
            dma((chips - 1,)),
            dma((parts - 1,)),
            dma((parts - 1,)),
            dma((parts - 1,)),
            dma((parts - 1,)),
            dma((docs - 1,)),
            dma((docs - 1,)),
        ],
        compiler_params=pltpu.CompilerParams(
            collective_id=0, has_side_effects=True, vmem_limit_bytes=56 * 2**20
        ),
    )(
        residual,
        norm_gain.reshape(1, -1),
        key_weight,
        value_weight,
        key_grad,
        value_grad,
        key_left,
        value_left,
        key_right,
        value_right,
        queries,
        doc_lengths,
    )
    return key_out, value_out, hidden_grad, jnp.sum(shares, axis=2)


def solution(mesh):
    in_specs = (
        P(("groups", "dp"), "tensor"),
        P("tensor"),
        P("tensor", None),
        P("tensor", None),
        P(("groups", "dp", "tensor"), None),
        P(("groups", "dp", "tensor"), None),
        P("tensor", None),
        P("tensor", None),
        P(),
        P(),
        P(("dp", "tensor"), None),
        P(("groups", "dp")),
    )
    out_specs = (
        P(("groups", "dp", "tensor"), None),
        P(("groups", "dp", "tensor"), None),
        P(("groups", "dp"), "tensor"),
        P("groups", ("dp", "tensor")),
    )
    return jax.shard_map(body, mesh=mesh, in_specs=in_specs, out_specs=out_specs, check_vma=False)
```

```python
import functools

import jax
import jax.numpy as jnp
from jax import lax
from jax.experimental import pallas as pl
from jax.experimental.pallas import tpu as pltpu
from jax.sharding import PartitionSpec as P

F32, BF16 = jnp.float32, jnp.bfloat16
LANES = 128


def kernel(
    parts,
    docs,
    residual,
    gain,
    key_weight,
    value_weight,
    key_grad,
    value_grad,
    key_left,
    value_left,
    key_right,
    value_right,
    queries,
    length,
    key_out,
    value_out,
    hidden_out,
    score_out,
    res_v,
    gain_v,
    kw_v,
    vw_v,
    left_w,
    kr_v,
    vr_v,
    got_k,
    got_v,
    mask_k,
    mask_v,
    partial,
    sib_in,
    x_out,
    x_in,
    left_t,
    squares,
    gram_rows,
    gram_in,
    flat_in,
    load_sem,
    res_sem,
    own_sem,
    ag_sib_s,
    ag_sib_r,
    ag_x_s,
    ag_x_r,
    ag_f_s,
    ag_f_r,
    rs_sib_s,
    rs_sib_r,
    rs_x_s,
    rs_x_r,
    sq_s,
    sq_r,
    gr_s,
    gr_r,
    fl_s,
    fl_r,
):
    chips = parts // 2
    slots, features = res_v.shape
    rows = slots // parts
    columns = kw_v.shape[1]
    rank = kr_v.shape[0]
    me = lax.axis_index("tensor")
    doc = lax.axis_index("dp")
    chip, core = me // 2, lax.rem(me, 2)
    sibling = chip * 2 + 1 - core

    def send(src, dst, s_sem, r_sem, target):
        return pltpu.make_async_remote_copy(
            src_ref=src,
            dst_ref=dst,
            send_sem=s_sem,
            recv_sem=r_sem,
            device_id=target,
            device_id_type=pl.DeviceIdType.MESH,
        )

    def chip_at(step):
        return lax.rem(chip + step + chips, chips)

    def block_of(order):
        step = lax.rem(order // 2 + 1, chips)
        other = lax.rem(order, 2)
        return chip_at(step) * 2 + jnp.where(other == 0, 1 - core, core)

    contract = (((1,), (1,)), ((), ()))

    loads = [
        pltpu.make_async_copy(src, dst, load_sem.at[i])
        for i, (src, dst) in enumerate(
            (
                (gain, gain_v),
                (key_weight, kw_v),
                (value_weight, vw_v),
                (key_left, left_w.at[:rank]),
                (value_left, left_w.at[rank:]),
                (key_right, kr_v),
                (value_right, vr_v),
            )
        )
    ]

    def res_copy(order):
        at = pl.ds(pl.multiple_of(block_of(order) * rows, rows), rows)
        return pltpu.make_async_copy(residual.at[at], res_v.at[at], res_sem.at[order])

    own_copies = [
        pltpu.make_async_copy(key_grad, got_k.at[me], own_sem.at[0]),
        pltpu.make_async_copy(value_grad, got_v.at[me], own_sem.at[1]),
    ]

    barrier = pltpu.get_barrier_semaphore()
    for step in range(1, parts):
        pl.semaphore_signal(
            barrier, inc=1, device_id={"tensor": lax.rem(me + step, parts)},
            device_id_type=pl.DeviceIdType.MESH,
        )

    def greet(step, carry):
        pl.semaphore_signal(
            barrier, inc=1, device_id={"dp": lax.rem(doc + step, docs)},
            device_id_type=pl.DeviceIdType.MESH,
        )
        return carry

    lax.fori_loop(1, docs, greet, 0)
    for copy in loads[:5]:
        copy.start()
    for order in range(parts):
        res_copy(order).start()
    for copy in loads[5:]:
        copy.start()
    for copy in own_copies:
        copy.start()
    pl.semaphore_wait(barrier, parts - 1 + docs - 1)

    grads = ((key_grad, got_k), (value_grad, got_v))
    ag_x = [
        [
            send(src, got.at[me], ag_x_s.at[step - 1, i], ag_x_r.at[step - 1, i],
                 {"tensor": chip_at(step) * 2 + core})
            for i, (src, got) in enumerate(grads)
        ]
        for step in range(1, chips)
    ]
    ag_sib = [
        send(src, got.at[me], ag_sib_s.at[i], ag_sib_r.at[i], {"tensor": sibling})
        for i, (src, got) in enumerate(grads)
    ]
    for pair in ag_x:
        for copy in pair:
            copy.start()
    for copy in ag_sib:
        copy.start()

    for copy in loads:
        copy.wait()

    def rs_sib(at):
        return send(partial.at[2 * at], sib_in.at[at], rs_sib_s.at[at], rs_sib_r.at[at],
                    {"tensor": sibling})

    def forward(order, carry):
        res_copy(order).wait()
        block = block_of(order)
        wide = res_v[pl.ds(pl.multiple_of(block * rows, rows), rows), :].astype(F32)
        scaled = (wide * gain_v[...]).astype(BF16)
        squared = wide * wide
        lane_sum = squared[:, :LANES]
        for i in range(1, features // LANES):
            lane_sum = lane_sum + squared[:, i * LANES : (i + 1) * LANES]
        squares[me, pl.ds(block, 1), :] = jnp.sum(lane_sum.T, axis=0, keepdims=True)
        partial[order, :, :columns] = jnp.dot(
            scaled, kw_v[...], preferred_element_type=F32
        ).astype(BF16)
        partial[order, :, columns:] = jnp.dot(
            scaled, vw_v[...], preferred_element_type=F32
        ).astype(BF16)
        left_t[block] = lax.dot_general(
            left_w[...], scaled, contract, preferred_element_type=F32
        )

        @pl.when(lax.rem(order, 2) == 0)
        def _():
            rs_sib(order // 2).start()

        return carry

    lax.fori_loop(0, parts, forward, 0)

    sq = [
        send(squares.at[me], squares.at[me], sq_s.at[step - 1], sq_r.at[step - 1],
             {"tensor": lax.rem(me + step, parts)})
        for step in range(1, parts)
    ]
    for copy in sq:
        copy.start()

    rs_x = []
    for step in range(1, chips):
        at = step - 1
        rs_sib(at).wait_recv()
        x_out[at] = (
            partial[2 * at + 1].astype(F32) + sib_in[at].astype(F32)
        ).astype(BF16)
        rs_x.append(
            send(x_out.at[at], x_in.at[at], rs_x_s.at[at], rs_x_r.at[at],
                 {"tensor": chip_at(step) * 2 + core})
        )

    def inverse_of(block):
        total = squares[0, pl.ds(block, 1), :]
        for i in range(1, parts):
            total = total + squares[i, pl.ds(block, 1), :]
        return lax.rsqrt(total / (features * parts) + 1e-05)

    span = 2 * rows
    tile = min(features, 512)

    def mask_chip(at):
        for half in range(2):
            block = at * 2 + half
            place = block * rows + lax.broadcasted_iota(jnp.int32, (rows, columns), 0)
            live = (place < length[0]).astype(F32).astype(BF16)
            mask_k[half * rows : (half + 1) * rows, :] = got_k[block] * live
            mask_v[half * rows : (half + 1) * rows, :] = got_v[block] * live

    def gram_add(at, first):
        right_k = lax.dot_general(
            mask_k[...], kr_v[...], contract, preferred_element_type=F32
        )
        right_v = lax.dot_general(
            mask_v[...], vr_v[...], contract, preferred_element_type=F32
        )
        for half in range(2):
            block = at * 2 + half
            left = left_t[block] * inverse_of(block)
            for i, right in enumerate((right_k, right_v)):
                term = jnp.dot(
                    left[i * rank : (i + 1) * rank],
                    right[half * rows : (half + 1) * rows],
                    precision=lax.Precision.HIGHEST,
                    preferred_element_type=F32,
                )
                here = slice(i * rank, (i + 1) * rank)
                if first and half == 0:
                    gram_rows[here, :] = term
                else:
                    gram_rows[here, :] += term

    def back(at):
        to = pl.ds(pl.multiple_of(at * span, span), span)

        def one(i, carry):
            here = pl.ds(pl.multiple_of(i * tile, tile), tile)
            total = lax.dot_general(
                mask_k[...], kw_v[here, :], contract, preferred_element_type=F32
            ) + lax.dot_general(
                mask_v[...], vw_v[here, :], contract, preferred_element_type=F32
            )
            hidden_out[to, here] = total.astype(BF16)
            return carry

        lax.fori_loop(0, features // tile, one, 0)

    for copy in own_copies:
        copy.wait()
    for copy in ag_sib:
        copy.wait_recv()
    mask_chip(chip)
    back(chip)
    for copy in sq:
        copy.wait_recv()
    gram_add(chip, True)

    for pair in ag_x:
        for copy in pair:
            copy.wait_send()
    for copy in rs_x:
        copy.start()
    passed = []
    for step in range(1, chips):
        origin = chip_at(-step) * 2 + core
        for i, (_, got) in enumerate(grads):
            ag_x[step - 1][i].wait_recv()
            copy = send(got.at[origin], got.at[origin], ag_f_s.at[step - 1, i],
                        ag_f_r.at[step - 1, i], {"tensor": sibling})
            copy.start()
            passed.append(copy)

    for step in range(1, chips):
        at = chip_at(-step)
        for i in range(2):
            passed[2 * (step - 1) + i].wait_recv()
        mask_chip(at)
        gram_add(at, False)
        if step == chips - 1:
            half = gram_rows.shape[0] // 2
            gram_in[me] = jnp.concatenate(
                [gram_rows[pl.ds(0, half, stride=2), :], gram_rows[pl.ds(1, half, stride=2), :]],
                axis=1,
            )
            gr = [
                send(gram_in.at[me], gram_in.at[me], gr_s.at[to - 1], gr_r.at[to - 1],
                     {"tensor": lax.rem(me + to, parts)})
                for to in range(1, parts)
            ]
            for copy in gr:
                copy.start()
        back(at)

    for copy in gr:
        copy.wait_recv()
    gram = gram_in[0]
    for i in range(1, parts):
        gram = gram + gram_in[i]
    flat_in[doc] = (gram / slots).astype(BF16)

    def flat_copy(step):
        return send(flat_in.at[doc], flat_in.at[doc], fl_s.at[step - 1], fl_r.at[step - 1],
                    {"dp": lax.rem(doc + step, docs)})

    def flat_start(step, carry):
        flat_copy(step).start()
        return carry

    def flat_wait(step, carry):
        flat_copy(step).wait()
        return carry

    lax.fori_loop(1, docs, flat_start, 0)

    last = chips - 1
    rs_sib(last).wait_recv()
    own = partial[2 * last + 1].astype(F32) + sib_in[last].astype(F32)
    inverse = jnp.broadcast_to(inverse_of(me), (LANES, rows)).T

    lax.fori_loop(1, docs, flat_wait, 0)

    def score(i, carry):
        flat = flat_in[i].astype(F32)
        total = jnp.zeros((queries.shape[0], LANES), F32)
        for j in range(flat.shape[0]):
            total = total + queries[:, j * LANES : (j + 1) * LANES].astype(F32) * flat[j : j + 1]
        score_out[i] = total
        return carry

    lax.fori_loop(0, docs, score, 0)

    for copy in rs_x:
        copy.wait_recv()
    for i in range(chips - 1):
        own = own + x_in[i].astype(F32)
    for i in range(columns // LANES):
        here = slice(i * LANES, (i + 1) * LANES)
        there = slice(columns + i * LANES, columns + (i + 1) * LANES)
        key_out[:, here] = (own[:, here] * inverse).astype(BF16)
        value_out[:, here] = (own[:, there] * inverse).astype(BF16)

    for copy in ag_sib + passed + sq + gr + rs_x:
        copy.wait_send()
    for i in range(chips):
        rs_sib(i).wait_send()


def finish(key_in, value_in, hidden_in, shares, key_out, value_out, hidden_out, scores, sem):
    copies = [
        pltpu.make_async_copy(src, dst, sem.at[i])
        for i, (src, dst) in enumerate(
            ((hidden_in, hidden_out), (key_in, key_out), (value_in, value_out))
        )
    ]
    for copy in copies:
        copy.start()
    scores[...] = jnp.sum(shares[...], axis=2)
    for copy in copies:
        copy.wait()


def body(
    residual,
    norm_gain,
    key_weight,
    value_weight,
    key_grad,
    value_grad,
    key_left,
    value_left,
    key_right,
    value_right,
    queries,
    doc_lengths,
):
    parts, docs = lax.axis_size("tensor"), lax.axis_size("dp")
    chips = parts // 2
    slots, features = residual.shape
    rows = slots // parts
    columns, rank = key_weight.shape[1], key_left.shape[1]
    hbm = pl.BlockSpec(memory_space=pl.ANY)
    vmem = pl.BlockSpec(memory_space=pltpu.VMEM)
    dma = pltpu.SemaphoreType.DMA
    flat_rows = 2 * rank * rank // LANES
    key_out, value_out, hidden_grad, shares = pl.pallas_call(
        functools.partial(kernel, parts, docs),
        out_shape=(
            pltpu.VMEM((rows, columns), BF16),
            pltpu.VMEM((rows, columns), BF16),
            pltpu.VMEM((slots, features), BF16),
            pltpu.VMEM((docs, queries.shape[0], LANES), F32),
        ),
        in_specs=[hbm] * 10 + [vmem, pl.BlockSpec(memory_space=pltpu.SMEM)],
        out_specs=(vmem,) * 4,
        scratch_shapes=[
            pltpu.VMEM((slots, features), BF16),
            pltpu.VMEM((1, features), F32),
            pltpu.VMEM((features, columns), BF16),
            pltpu.VMEM((features, columns), BF16),
            pltpu.VMEM((2 * rank, features), BF16),
            pltpu.VMEM((rank, columns), BF16),
            pltpu.VMEM((rank, columns), BF16),
            pltpu.VMEM((parts, rows, columns), BF16),
            pltpu.VMEM((parts, rows, columns), BF16),
            pltpu.VMEM((2 * rows, columns), BF16),
            pltpu.VMEM((2 * rows, columns), BF16),
            pltpu.VMEM((parts, rows, 2 * columns), BF16),
            pltpu.VMEM((chips, rows, 2 * columns), BF16),
            pltpu.VMEM((chips - 1, rows, 2 * columns), BF16),
            pltpu.VMEM((chips - 1, rows, 2 * columns), BF16),
            pltpu.VMEM((parts, 2 * rank, rows), F32),
            pltpu.VMEM((parts, parts, rows), F32),
            pltpu.VMEM((2 * rank, rank), F32),
            pltpu.VMEM((parts, flat_rows, LANES), F32),
            pltpu.VMEM((docs, flat_rows, LANES), BF16),
            dma((7,)),
            dma((parts,)),
            dma((2,)),
            dma((2,)),
            dma((2,)),
            dma((chips - 1, 2)),
            dma((chips - 1, 2)),
            dma((chips - 1, 2)),
            dma((chips - 1, 2)),
            dma((chips,)),
            dma((chips,)),
            dma((chips - 1,)),
            dma((chips - 1,)),
            dma((parts - 1,)),
            dma((parts - 1,)),
            dma((parts - 1,)),
            dma((parts - 1,)),
            dma((docs - 1,)),
            dma((docs - 1,)),
        ],
        compiler_params=pltpu.CompilerParams(
            collective_id=0, has_side_effects=True, vmem_limit_bytes=58 * 2**20
        ),
    )(
        residual,
        norm_gain.reshape(1, -1),
        key_weight,
        value_weight,
        key_grad,
        value_grad,
        key_left.T,
        value_left.T,
        key_right.T,
        value_right.T,
        queries,
        doc_lengths,
    )
    return pl.pallas_call(
        finish,
        out_shape=(
            jax.ShapeDtypeStruct((rows, columns), BF16),
            jax.ShapeDtypeStruct((rows, columns), BF16),
            jax.ShapeDtypeStruct((slots, features), BF16),
            jax.ShapeDtypeStruct((docs, queries.shape[0]), F32),
        ),
        in_specs=[vmem] * 4,
        out_specs=(hbm, hbm, hbm, vmem),
        scratch_shapes=[dma((3,))],
        compiler_params=pltpu.CompilerParams(vmem_limit_bytes=2 * 2**20),
    )(key_out, value_out, hidden_grad, shares)


def solution(mesh):
    in_specs = (
        P(("groups", "dp"), "tensor"),
        P("tensor"),
        P("tensor", None),
        P("tensor", None),
        P(("groups", "dp", "tensor"), None),
        P(("groups", "dp", "tensor"), None),
        P("tensor", None),
        P("tensor", None),
        P(),
        P(),
        P(("dp", "tensor"), None),
        P(("groups", "dp")),
    )
    out_specs = (
        P(("groups", "dp", "tensor"), None),
        P(("groups", "dp", "tensor"), None),
        P(("groups", "dp"), "tensor"),
        P("groups", ("dp", "tensor")),
    )
    return jax.shard_map(body, mesh=mesh, in_specs=in_specs, out_specs=out_specs, check_vma=False)
```

```python
import functools

import jax
import jax.numpy as jnp
from jax import lax
from jax.experimental import pallas as pl
from jax.experimental.pallas import tpu as pltpu
from jax.sharding import PartitionSpec as P

F32, BF16 = jnp.float32, jnp.bfloat16
LANES = 128
PIECES = 4
SPLIT = 8


def kernel(
    parts,
    docs,
    residual,
    gain,
    key_weight,
    value_weight,
    key_grad,
    value_grad,
    key_left,
    value_left,
    key_right,
    value_right,
    queries,
    length,
    key_out,
    value_out,
    hidden_out,
    score_out,
    res_v,
    gain_v,
    kw_v,
    vw_v,
    left_w,
    kr_v,
    vr_v,
    got_k,
    got_v,
    mask_k,
    mask_v,
    partial,
    sib_in,
    x_out,
    x_in,
    left_t,
    squares,
    gram_rows,
    gram_in,
    flat_in,
    load_sem,
    res_sem,
    own_sem,
    ag_sib_s,
    ag_sib_r,
    ag_x_s,
    ag_x_r,
    ag_f_s,
    ag_f_r,
    rs_sib_s,
    rs_sib_r,
    rs_x_s,
    rs_x_r,
    sq_s,
    sq_r,
    gr_s,
    gr_r,
    fl_s,
    fl_r,
):
    chips = parts // 2
    slots, features = res_v.shape
    rows = slots // parts
    columns = kw_v.shape[1]
    rank = kr_v.shape[0]
    me = lax.axis_index("tensor")
    doc = lax.axis_index("dp")
    chip, core = me // 2, lax.rem(me, 2)
    sibling = chip * 2 + 1 - core

    def send(src, dst, s_sem, r_sem, target):
        return pltpu.make_async_remote_copy(
            src_ref=src,
            dst_ref=dst,
            send_sem=s_sem,
            recv_sem=r_sem,
            device_id=target,
            device_id_type=pl.DeviceIdType.MESH,
        )

    def chip_at(step):
        return lax.rem(chip + step + chips, chips)

    def block_of(order):
        step = lax.rem(order // 2 + 1, chips)
        other = lax.rem(order, 2)
        return chip_at(step) * 2 + jnp.where(other == 0, 1 - core, core)

    contract = (((1,), (1,)), ((), ()))

    loads = [
        pltpu.make_async_copy(src, dst, load_sem.at[i])
        for i, (src, dst) in enumerate(
            (
                (gain, gain_v),
                (key_weight, kw_v),
                (value_weight, vw_v),
                (key_left, left_w.at[:rank]),
                (value_left, left_w.at[rank:]),
                (key_right, kr_v),
                (value_right, vr_v),
            )
        )
    ]

    def res_copy(order):
        at = pl.ds(pl.multiple_of(block_of(order) * rows, rows), rows)
        return pltpu.make_async_copy(residual.at[at], res_v.at[at], res_sem.at[order])

    own_copies = [
        pltpu.make_async_copy(key_grad, got_k.at[me], own_sem.at[0]),
        pltpu.make_async_copy(value_grad, got_v.at[me], own_sem.at[1]),
    ]

    barrier = pltpu.get_barrier_semaphore()
    for step in range(1, parts):
        pl.semaphore_signal(
            barrier, inc=1, device_id={"tensor": lax.rem(me + step, parts)},
            device_id_type=pl.DeviceIdType.MESH,
        )

    def greet(step, carry):
        pl.semaphore_signal(
            barrier, inc=1, device_id={"dp": lax.rem(doc + step, docs)},
            device_id_type=pl.DeviceIdType.MESH,
        )
        return carry

    lax.fori_loop(1, docs, greet, 0)
    for copy in loads[:5]:
        copy.start()
    for order in range(parts):
        res_copy(order).start()
    for copy in loads[5:]:
        copy.start()
    for copy in own_copies:
        copy.start()
    pl.semaphore_wait(barrier, parts - 1 + docs - 1)

    grads = ((key_grad, got_k), (value_grad, got_v))
    ag_x = [
        [
            send(src, got.at[me], ag_x_s.at[step - 1, i], ag_x_r.at[step - 1, i],
                 {"tensor": chip_at(step) * 2 + core})
            for i, (src, got) in enumerate(grads)
        ]
        for step in range(1, chips)
    ]
    ag_sib = [
        send(src, got.at[me], ag_sib_s.at[i], ag_sib_r.at[i], {"tensor": sibling})
        for i, (src, got) in enumerate(grads)
    ]
    for pair in ag_x:
        for copy in pair:
            copy.start()
    for copy in ag_sib:
        copy.start()

    for copy in loads:
        copy.wait()

    def rs_sib(at):
        return send(partial.at[2 * at], sib_in.at[at], rs_sib_s.at[at], rs_sib_r.at[at],
                    {"tensor": sibling})

    def forward(order, carry):
        res_copy(order).wait()
        block = block_of(order)
        wide = res_v[pl.ds(pl.multiple_of(block * rows, rows), rows), :].astype(F32)
        scaled = (wide * gain_v[...]).astype(BF16)
        squared = wide * wide
        lane_sum = squared[:, :LANES]
        for i in range(1, features // LANES):
            lane_sum = lane_sum + squared[:, i * LANES : (i + 1) * LANES]
        squares[me, pl.ds(block, 1), :] = jnp.sum(lane_sum.T, axis=0, keepdims=True)
        partial[order, :, :columns] = jnp.dot(
            scaled, kw_v[...], preferred_element_type=F32
        ).astype(BF16)
        partial[order, :, columns:] = jnp.dot(
            scaled, vw_v[...], preferred_element_type=F32
        ).astype(BF16)
        left_t[block] = lax.dot_general(
            left_w[...], scaled, contract, preferred_element_type=F32
        )

        @pl.when(lax.rem(order, 2) == 0)
        def _():
            rs_sib(order // 2).start()

        return carry

    lax.fori_loop(0, parts, forward, 0)

    sq = [
        send(squares.at[me], squares.at[me], sq_s.at[step - 1], sq_r.at[step - 1],
             {"tensor": lax.rem(me + step, parts)})
        for step in range(1, parts)
    ]
    for copy in sq:
        copy.start()

    size = rows // PIECES
    pieces = [slice(i * size, (i + 1) * size) for i in range(PIECES)]
    rs_x = []
    for step in range(1, chips):
        at = step - 1
        rs_sib(at).wait_recv()
        x_out[at] = (
            partial[2 * at + 1].astype(F32) + sib_in[at].astype(F32)
        ).astype(BF16)
        rs_x.append(
            [
                send(x_out.at[at, here], x_in.at[at, here], rs_x_s.at[at, i], rs_x_r.at[at, i],
                     {"tensor": chip_at(step) * 2 + core})
                for i, here in enumerate(pieces)
            ]
        )

    def inverse_of(block):
        total = squares[0, pl.ds(block, 1), :]
        for i in range(1, parts):
            total = total + squares[i, pl.ds(block, 1), :]
        return lax.rsqrt(total / (features * parts) + 1e-05)

    span = 2 * rows
    tile = min(features, 512)

    def mask_chip(at):
        for half in range(2):
            block = at * 2 + half
            place = block * rows + lax.broadcasted_iota(jnp.int32, (rows, columns), 0)
            live = (place < length[0]).astype(F32).astype(BF16)
            mask_k[half * rows : (half + 1) * rows, :] = got_k[block] * live
            mask_v[half * rows : (half + 1) * rows, :] = got_v[block] * live

    def gram_add(at, first):
        right_k = lax.dot_general(
            mask_k[...], kr_v[...], contract, preferred_element_type=F32
        )
        right_v = lax.dot_general(
            mask_v[...], vr_v[...], contract, preferred_element_type=F32
        )
        for half in range(2):
            block = at * 2 + half
            left = left_t[block] * inverse_of(block)
            for i, right in enumerate((right_k, right_v)):
                term = jnp.dot(
                    left[i * rank : (i + 1) * rank],
                    right[half * rows : (half + 1) * rows],
                    precision=lax.Precision.HIGHEST,
                    preferred_element_type=F32,
                )
                here = slice(i * rank, (i + 1) * rank)
                if first and half == 0:
                    gram_rows[here, :] = term
                else:
                    gram_rows[here, :] += term

    def back(at):
        to = pl.ds(pl.multiple_of(at * span, span), span)

        def one(i, carry):
            here = pl.ds(pl.multiple_of(i * tile, tile), tile)
            total = lax.dot_general(
                mask_k[...], kw_v[here, :], contract, preferred_element_type=F32
            ) + lax.dot_general(
                mask_v[...], vw_v[here, :], contract, preferred_element_type=F32
            )
            hidden_out[to, here] = total.astype(BF16)
            return carry

        lax.fori_loop(0, features // tile, one, 0)

    for copy in own_copies:
        copy.wait()
    for copy in ag_sib:
        copy.wait_recv()
    mask_chip(chip)
    back(chip)
    for copy in sq:
        copy.wait_recv()
    gram_add(chip, True)

    for pair in ag_x:
        for copy in pair:
            copy.wait_send()
    for group in rs_x:
        group[0].start()
    passed = []
    for step in range(1, chips):
        origin = chip_at(-step) * 2 + core
        for i, (_, got) in enumerate(grads):
            ag_x[step - 1][i].wait_recv()
            copy = send(got.at[origin], got.at[origin], ag_f_s.at[step - 1, i],
                        ag_f_r.at[step - 1, i], {"tensor": sibling})
            copy.start()
            passed.append(copy)

    for step in range(1, chips):
        at = chip_at(-step)
        for i in range(2):
            passed[2 * (step - 1) + i].wait_recv()
        if step == chips - 1:
            for group in rs_x:
                group[1].start()
        mask_chip(at)
        gram_add(at, False)
        if step == chips - 1:
            half = gram_rows.shape[0] // 2
            gram_in[me] = jnp.concatenate(
                [gram_rows[pl.ds(0, half, stride=2), :], gram_rows[pl.ds(1, half, stride=2), :]],
                axis=1,
            )
            gr = [
                send(gram_in.at[me], gram_in.at[me], gr_s.at[to - 1], gr_r.at[to - 1],
                     {"tensor": lax.rem(me + to, parts)})
                for to in range(1, parts)
            ]
            for copy in gr:
                copy.start()
            for i in range(2, PIECES):
                for group in rs_x:
                    group[i].start()
        back(at)

    for copy in gr:
        copy.wait_recv()
    gram = gram_in[0]
    for i in range(1, parts):
        gram = gram + gram_in[i]
    flat_in[doc] = (gram / slots).astype(BF16)

    def flat_copy(step):
        return send(flat_in.at[doc], flat_in.at[doc], fl_s.at[step - 1], fl_r.at[step - 1],
                    {"dp": lax.rem(doc + step, docs)})

    def flat_start(step, carry):
        flat_copy(step).start()
        return carry

    def flat_wait(step, carry):
        flat_copy(step).wait()
        return carry

    lax.fori_loop(1, docs, flat_start, 0)

    last = chips - 1
    rs_sib(last).wait_recv()
    inverse = jnp.broadcast_to(inverse_of(me), (LANES, rows)).T

    lax.fori_loop(1, docs, flat_wait, 0)

    def score(i, carry):
        flat = flat_in[i].astype(F32)
        total = jnp.zeros((queries.shape[0], LANES), F32)
        for j in range(flat.shape[0]):
            total = total + queries[:, j * LANES : (j + 1) * LANES].astype(F32) * flat[j : j + 1]
        score_out[i] = total
        return carry

    lax.fori_loop(0, docs, score, 0)

    for at, piece in enumerate(pieces):
        for group in rs_x:
            group[at].wait_recv()
        own = partial[2 * last + 1, piece].astype(F32) + sib_in[last, piece].astype(F32)
        for i in range(chips - 1):
            own = own + x_in[i, piece].astype(F32)
        scale = inverse[piece]
        for i in range(columns // LANES):
            here = slice(i * LANES, (i + 1) * LANES)
            there = slice(columns + i * LANES, columns + (i + 1) * LANES)
            key_out[piece, here] = (own[:, here] * scale).astype(BF16)
            value_out[piece, here] = (own[:, there] * scale).astype(BF16)

    for copy in ag_sib + passed + sq + gr + [copy for group in rs_x for copy in group]:
        copy.wait_send()
    for i in range(chips):
        rs_sib(i).wait_send()


def finish(key_in, value_in, hidden_in, shares, key_out, value_out, hidden_out, scores, sem):
    size = hidden_in.shape[0] // SPLIT
    views = [slice(i * size, (i + 1) * size) for i in range(SPLIT)]
    pairs = [(hidden_in.at[here], hidden_out.at[here]) for here in views]
    pairs += [(key_in, key_out), (value_in, value_out)]
    copies = [
        pltpu.make_async_copy(src, dst, sem.at[i]) for i, (src, dst) in enumerate(pairs)
    ]
    for copy in copies:
        copy.start()
    scores[...] = jnp.sum(shares[...], axis=2)
    for copy in copies:
        copy.wait()


def body(
    residual,
    norm_gain,
    key_weight,
    value_weight,
    key_grad,
    value_grad,
    key_left,
    value_left,
    key_right,
    value_right,
    queries,
    doc_lengths,
):
    parts, docs = lax.axis_size("tensor"), lax.axis_size("dp")
    chips = parts // 2
    slots, features = residual.shape
    rows = slots // parts
    columns, rank = key_weight.shape[1], key_left.shape[1]
    hbm = pl.BlockSpec(memory_space=pl.ANY)
    vmem = pl.BlockSpec(memory_space=pltpu.VMEM)
    dma = pltpu.SemaphoreType.DMA
    flat_rows = 2 * rank * rank // LANES
    key_out, value_out, hidden_grad, shares = pl.pallas_call(
        functools.partial(kernel, parts, docs),
        out_shape=(
            pltpu.VMEM((rows, columns), BF16),
            pltpu.VMEM((rows, columns), BF16),
            pltpu.VMEM((slots, features), BF16),
            pltpu.VMEM((docs, queries.shape[0], LANES), F32),
        ),
        in_specs=[hbm] * 10 + [vmem, pl.BlockSpec(memory_space=pltpu.SMEM)],
        out_specs=(vmem,) * 4,
        scratch_shapes=[
            pltpu.VMEM((slots, features), BF16),
            pltpu.VMEM((1, features), F32),
            pltpu.VMEM((features, columns), BF16),
            pltpu.VMEM((features, columns), BF16),
            pltpu.VMEM((2 * rank, features), BF16),
            pltpu.VMEM((rank, columns), BF16),
            pltpu.VMEM((rank, columns), BF16),
            pltpu.VMEM((parts, rows, columns), BF16),
            pltpu.VMEM((parts, rows, columns), BF16),
            pltpu.VMEM((2 * rows, columns), BF16),
            pltpu.VMEM((2 * rows, columns), BF16),
            pltpu.VMEM((parts, rows, 2 * columns), BF16),
            pltpu.VMEM((chips, rows, 2 * columns), BF16),
            pltpu.VMEM((chips - 1, rows, 2 * columns), BF16),
            pltpu.VMEM((chips - 1, rows, 2 * columns), BF16),
            pltpu.VMEM((parts, 2 * rank, rows), F32),
            pltpu.VMEM((parts, parts, rows), F32),
            pltpu.VMEM((2 * rank, rank), F32),
            pltpu.VMEM((parts, flat_rows, LANES), F32),
            pltpu.VMEM((docs, flat_rows, LANES), BF16),
            dma((7,)),
            dma((parts,)),
            dma((2,)),
            dma((2,)),
            dma((2,)),
            dma((chips - 1, 2)),
            dma((chips - 1, 2)),
            dma((chips - 1, 2)),
            dma((chips - 1, 2)),
            dma((chips,)),
            dma((chips,)),
            dma((chips - 1, PIECES)),
            dma((chips - 1, PIECES)),
            dma((parts - 1,)),
            dma((parts - 1,)),
            dma((parts - 1,)),
            dma((parts - 1,)),
            dma((docs - 1,)),
            dma((docs - 1,)),
        ],
        compiler_params=pltpu.CompilerParams(
            collective_id=0, has_side_effects=True, vmem_limit_bytes=58 * 2**20
        ),
    )(
        residual,
        norm_gain.reshape(1, -1),
        key_weight,
        value_weight,
        key_grad,
        value_grad,
        key_left.T,
        value_left.T,
        key_right.T,
        value_right.T,
        queries,
        doc_lengths,
    )
    return pl.pallas_call(
        finish,
        out_shape=(
            jax.ShapeDtypeStruct((rows, columns), BF16),
            jax.ShapeDtypeStruct((rows, columns), BF16),
            jax.ShapeDtypeStruct((slots, features), BF16),
            jax.ShapeDtypeStruct((docs, queries.shape[0]), F32),
        ),
        in_specs=[vmem] * 4,
        out_specs=(hbm, hbm, hbm, vmem),
        scratch_shapes=[dma((SPLIT + 2,))],
        compiler_params=pltpu.CompilerParams(vmem_limit_bytes=2 * 2**20),
    )(key_out, value_out, hidden_grad, shares)


def solution(mesh):
    in_specs = (
        P(("groups", "dp"), "tensor"),
        P("tensor"),
        P("tensor", None),
        P("tensor", None),
        P(("groups", "dp", "tensor"), None),
        P(("groups", "dp", "tensor"), None),
        P("tensor", None),
        P("tensor", None),
        P(),
        P(),
        P(("dp", "tensor"), None),
        P(("groups", "dp")),
    )
    out_specs = (
        P(("groups", "dp", "tensor"), None),
        P(("groups", "dp", "tensor"), None),
        P(("groups", "dp"), "tensor"),
        P("groups", ("dp", "tensor")),
    )
    return jax.shard_map(body, mesh=mesh, in_specs=in_specs, out_specs=out_specs, check_vma=False)
```

```python
import functools

import jax
import jax.numpy as jnp
from jax import lax
from jax.experimental import pallas as pl
from jax.experimental.pallas import tpu as pltpu
from jax.sharding import PartitionSpec as P

F32, BF16 = jnp.float32, jnp.bfloat16
LANES = 128
PIECES = 4
SPLIT = 8


def kernel(
    parts,
    docs,
    residual,
    gain,
    key_weight,
    value_weight,
    key_grad,
    value_grad,
    key_left,
    value_left,
    key_right,
    value_right,
    queries,
    length,
    key_out,
    value_out,
    hidden_out,
    score_out,
    res_v,
    gain_v,
    kw_v,
    vw_v,
    left_w,
    kr_v,
    vr_v,
    got_k,
    got_v,
    mask_k,
    mask_v,
    partial,
    sib_in,
    x_out,
    x_in,
    left_t,
    right_g,
    squares,
    gram_rows,
    gram_in,
    flat_in,
    load_sem,
    res_sem,
    own_sem,
    ag_sib_s,
    ag_sib_r,
    ag_x_s,
    ag_x_r,
    ag_f_s,
    ag_f_r,
    rs_sib_s,
    rs_sib_r,
    rs_x_s,
    rs_x_r,
    sq_s,
    sq_r,
    gr_s,
    gr_r,
    fl_s,
    fl_r,
    rt_s,
    rt_r,
):
    chips = parts // 2
    slots, features = res_v.shape
    rows = slots // parts
    columns = kw_v.shape[1]
    rank = kr_v.shape[0]
    me = lax.axis_index("tensor")
    doc = lax.axis_index("dp")
    chip, core = me // 2, lax.rem(me, 2)
    sibling = chip * 2 + 1 - core

    def send(src, dst, s_sem, r_sem, target):
        return pltpu.make_async_remote_copy(
            src_ref=src,
            dst_ref=dst,
            send_sem=s_sem,
            recv_sem=r_sem,
            device_id=target,
            device_id_type=pl.DeviceIdType.MESH,
        )

    def chip_at(step):
        return lax.rem(chip + step + chips, chips)

    def block_of(order):
        step = lax.rem(order // 2 + 1, chips)
        other = lax.rem(order, 2)
        return chip_at(step) * 2 + jnp.where(other == 0, 1 - core, core)

    contract = (((1,), (1,)), ((), ()))

    loads = [
        pltpu.make_async_copy(src, dst, load_sem.at[i])
        for i, (src, dst) in enumerate(
            (
                (gain, gain_v),
                (key_weight, kw_v),
                (value_weight, vw_v),
                (key_left, left_w.at[:rank]),
                (value_left, left_w.at[rank:]),
                (key_right, kr_v),
                (value_right, vr_v),
            )
        )
    ]

    def res_copy(order):
        at = pl.ds(pl.multiple_of(block_of(order) * rows, rows), rows)
        return pltpu.make_async_copy(residual.at[at], res_v.at[at], res_sem.at[order])

    own_copies = [
        pltpu.make_async_copy(key_grad, got_k.at[me], own_sem.at[0]),
        pltpu.make_async_copy(value_grad, got_v.at[me], own_sem.at[1]),
    ]

    barrier = pltpu.get_barrier_semaphore()
    for step in range(1, parts):
        pl.semaphore_signal(
            barrier, inc=1, device_id={"tensor": lax.rem(me + step, parts)},
            device_id_type=pl.DeviceIdType.MESH,
        )

    def greet(step, carry):
        pl.semaphore_signal(
            barrier, inc=1, device_id={"dp": lax.rem(doc + step, docs)},
            device_id_type=pl.DeviceIdType.MESH,
        )
        return carry

    lax.fori_loop(1, docs, greet, 0)
    for order in range(parts):
        res_copy(order).start()
    for copy in own_copies + loads[5:] + loads[:5]:
        copy.start()

    def square(order, carry):
        res_copy(order).wait()
        block = block_of(order)
        wide = res_v[pl.ds(pl.multiple_of(block * rows, rows), rows), :].astype(F32)
        squared = wide * wide
        lane_sum = squared[:, :LANES]
        for i in range(1, features // LANES):
            lane_sum = lane_sum + squared[:, i * LANES : (i + 1) * LANES]
        squares[me, pl.ds(block, 1), :] = jnp.sum(lane_sum.T, axis=0, keepdims=True)
        return carry

    lax.fori_loop(0, parts, square, 0)
    pl.semaphore_wait(barrier, parts - 1 + docs - 1)

    grads = ((key_grad, got_k), (value_grad, got_v))
    ag_x = [
        [
            send(src, got.at[me], ag_x_s.at[step - 1, i], ag_x_r.at[step - 1, i],
                 {"tensor": chip_at(step) * 2 + core})
            for i, (src, got) in enumerate(grads)
        ]
        for step in range(1, chips)
    ]
    ag_sib = [
        send(src, got.at[me], ag_sib_s.at[i], ag_sib_r.at[i], {"tensor": sibling})
        for i, (src, got) in enumerate(grads)
    ]
    sq = [
        send(squares.at[me], squares.at[me], sq_s.at[step - 1], sq_r.at[step - 1],
             {"tensor": lax.rem(me + step, parts)})
        for step in range(1, parts)
    ]
    for pair in ag_x:
        pair[0].start()
    for copy in sq:
        copy.start()
    for copy in own_copies + loads[5:]:
        copy.wait()

    def masked(block, got):
        place = block * rows + lax.broadcasted_iota(jnp.int32, (rows, columns), 0)
        return got[block] * (place < length[0]).astype(F32).astype(BF16)

    for i, (got, right) in enumerate(((got_k, kr_v), (got_v, vr_v))):
        right_g[me, :, i * rank : (i + 1) * rank] = lax.dot_general(
            masked(me, got), right[...], contract, preferred_element_type=F32
        ).astype(BF16)
    def right_send(block, at, target):
        return send(right_g.at[block], right_g.at[block], rt_s.at[at], rt_r.at[at],
                    {"tensor": target})

    rt_x = [
        right_send(me, step - 1, chip_at(step) * 2 + core) for step in range(1, chips)
    ]
    rt_sib = right_send(me, chips - 1, sibling)
    for copy in rt_x + [rt_sib]:
        copy.start()

    for pair in ag_x:
        pair[1].start()
    for copy in ag_sib:
        copy.start()

    for copy in loads[:5]:
        copy.wait()

    def rs_sib(at):
        return send(partial.at[2 * at], sib_in.at[at], rs_sib_s.at[at], rs_sib_r.at[at],
                    {"tensor": sibling})

    def forward(order, carry):
        block = block_of(order)
        wide = res_v[pl.ds(pl.multiple_of(block * rows, rows), rows), :].astype(F32)
        scaled = (wide * gain_v[...]).astype(BF16)
        partial[order, :, :columns] = jnp.dot(
            scaled, kw_v[...], preferred_element_type=F32
        ).astype(BF16)
        partial[order, :, columns:] = jnp.dot(
            scaled, vw_v[...], preferred_element_type=F32
        ).astype(BF16)
        left_t[block] = lax.dot_general(
            left_w[...], scaled, contract, preferred_element_type=F32
        )

        @pl.when(lax.rem(order, 2) == 0)
        def _():
            rs_sib(order // 2).start()

        return carry

    lax.fori_loop(0, parts, forward, 0)

    rt_pass = []
    for step in range(1, chips):
        rt_x[step - 1].wait_recv()
        origin = chip_at(-step) * 2 + core
        rt_pass.append(right_send(origin, chips - 1 + step, sibling))
        rt_pass[-1].start()

    size = rows // PIECES
    pieces = [slice(i * size, (i + 1) * size) for i in range(PIECES)]
    rs_x = []
    for step in range(1, chips):
        at = step - 1
        rs_sib(at).wait_recv()
        x_out[at] = (
            partial[2 * at + 1].astype(F32) + sib_in[at].astype(F32)
        ).astype(BF16)
        rs_x.append(
            [
                send(x_out.at[at, here], x_in.at[at, here], rs_x_s.at[at, i], rs_x_r.at[at, i],
                     {"tensor": chip_at(step) * 2 + core})
                for i, here in enumerate(pieces)
            ]
        )

    def inverse_of(block):
        total = squares[0, pl.ds(block, 1), :]
        for i in range(1, parts):
            total = total + squares[i, pl.ds(block, 1), :]
        return lax.rsqrt(total / (features * parts) + 1e-05)

    span = 2 * rows
    tile = min(features, 512)

    def mask_chip(at):
        for half in range(2):
            block = at * 2 + half
            mask_k[half * rows : (half + 1) * rows, :] = masked(block, got_k)
            mask_v[half * rows : (half + 1) * rows, :] = masked(block, got_v)

    def gram_share():
        def add(block, total):
            left = left_t[block] * inverse_of(block)
            right = right_g[block].astype(F32)
            return tuple(
                was
                + jnp.dot(
                    left[i * rank : (i + 1) * rank],
                    right[:, i * rank : (i + 1) * rank],
                    precision=lax.Precision.HIGHEST,
                    preferred_element_type=F32,
                )
                for i, was in enumerate(total)
            )

        zero = jnp.zeros((rank, rank), F32)
        for i, share in enumerate(lax.fori_loop(0, parts, add, (zero, zero))):
            gram_rows[i * rank : (i + 1) * rank, :] = share

    def back(at):
        to = pl.ds(pl.multiple_of(at * span, span), span)

        def one(i, carry):
            here = pl.ds(pl.multiple_of(i * tile, tile), tile)
            total = lax.dot_general(
                mask_k[...], kw_v[here, :], contract, preferred_element_type=F32
            ) + lax.dot_general(
                mask_v[...], vw_v[here, :], contract, preferred_element_type=F32
            )
            hidden_out[to, here] = total.astype(BF16)
            return carry

        lax.fori_loop(0, features // tile, one, 0)

    for copy in sq + [rt_sib] + rt_pass:
        copy.wait_recv()
    gram_share()
    half = gram_rows.shape[0] // 2
    gram_in[me] = jnp.concatenate(
        [gram_rows[pl.ds(0, half, stride=2), :], gram_rows[pl.ds(1, half, stride=2), :]],
        axis=1,
    ).astype(BF16)
    gr = [
        send(gram_in.at[me], gram_in.at[me], gr_s.at[to - 1], gr_r.at[to - 1],
             {"tensor": lax.rem(me + to, parts)})
        for to in range(1, parts)
    ]
    for copy in gr:
        copy.start()

    for i in range(PIECES):
        for group in rs_x:
            group[i].start()

    for copy in ag_sib:
        copy.wait_recv()
    mask_chip(chip)
    back(chip)

    passed = []
    for step in range(1, chips):
        origin = chip_at(-step) * 2 + core
        for i, (_, got) in enumerate(grads):
            ag_x[step - 1][i].wait_recv()
            copy = send(got.at[origin], got.at[origin], ag_f_s.at[step - 1, i],
                        ag_f_r.at[step - 1, i], {"tensor": sibling})
            copy.start()
            passed.append(copy)

    for copy in gr:
        copy.wait_recv()
    gram = gram_in[0].astype(F32)
    for i in range(1, parts):
        gram = gram + gram_in[i].astype(F32)
    flat_in[doc] = (gram / slots).astype(BF16)

    def flat_copy(step):
        return send(flat_in.at[doc], flat_in.at[doc], fl_s.at[step - 1], fl_r.at[step - 1],
                    {"dp": lax.rem(doc + step, docs)})

    def flat_start(step, carry):
        flat_copy(step).start()
        return carry

    def flat_wait(step, carry):
        flat_copy(step).wait()
        return carry

    lax.fori_loop(1, docs, flat_start, 0)

    for step in range(1, chips):
        for i in range(2):
            passed[2 * (step - 1) + i].wait_recv()
        mask_chip(chip_at(-step))
        back(chip_at(-step))

    last = chips - 1
    rs_sib(last).wait_recv()
    inverse = jnp.broadcast_to(inverse_of(me), (LANES, rows)).T

    lax.fori_loop(1, docs, flat_wait, 0)

    def score(i, carry):
        flat = flat_in[i].astype(F32)
        total = jnp.zeros((queries.shape[0], LANES), F32)
        for j in range(flat.shape[0]):
            total = total + queries[:, j * LANES : (j + 1) * LANES].astype(F32) * flat[j : j + 1]
        score_out[i] = total
        return carry

    lax.fori_loop(0, docs, score, 0)

    for at, piece in enumerate(pieces):
        for group in rs_x:
            group[at].wait_recv()
        own = partial[2 * last + 1, piece].astype(F32) + sib_in[last, piece].astype(F32)
        for i in range(chips - 1):
            own = own + x_in[i, piece].astype(F32)
        scale = inverse[piece]
        for i in range(columns // LANES):
            here = slice(i * LANES, (i + 1) * LANES)
            there = slice(columns + i * LANES, columns + (i + 1) * LANES)
            key_out[piece, here] = (own[:, here] * scale).astype(BF16)
            value_out[piece, here] = (own[:, there] * scale).astype(BF16)

    for copy in rt_x + [rt_sib] + rt_pass + ag_sib + [copy for pair in ag_x for copy in pair] + passed + sq + gr + [copy for group in rs_x for copy in group]:
        copy.wait_send()
    for i in range(chips):
        rs_sib(i).wait_send()


def finish(key_in, value_in, hidden_in, shares, key_out, value_out, hidden_out, scores, sem):
    size = hidden_in.shape[0] // SPLIT
    views = [slice(i * size, (i + 1) * size) for i in range(SPLIT)]
    pairs = [(hidden_in.at[here], hidden_out.at[here]) for here in views]
    pairs += [(key_in, key_out), (value_in, value_out)]
    copies = [
        pltpu.make_async_copy(src, dst, sem.at[i]) for i, (src, dst) in enumerate(pairs)
    ]
    for copy in copies:
        copy.start()
    scores[...] = jnp.sum(shares[...], axis=2)
    for copy in copies:
        copy.wait()


def body(
    residual,
    norm_gain,
    key_weight,
    value_weight,
    key_grad,
    value_grad,
    key_left,
    value_left,
    key_right,
    value_right,
    queries,
    doc_lengths,
):
    parts, docs = lax.axis_size("tensor"), lax.axis_size("dp")
    chips = parts // 2
    slots, features = residual.shape
    rows = slots // parts
    columns, rank = key_weight.shape[1], key_left.shape[1]
    hbm = pl.BlockSpec(memory_space=pl.ANY)
    vmem = pl.BlockSpec(memory_space=pltpu.VMEM)
    dma = pltpu.SemaphoreType.DMA
    flat_rows = 2 * rank * rank // LANES
    key_out, value_out, hidden_grad, shares = pl.pallas_call(
        functools.partial(kernel, parts, docs),
        out_shape=(
            pltpu.VMEM((rows, columns), BF16),
            pltpu.VMEM((rows, columns), BF16),
            pltpu.VMEM((slots, features), BF16),
            pltpu.VMEM((docs, queries.shape[0], LANES), F32),
        ),
        in_specs=[hbm] * 10 + [vmem, pl.BlockSpec(memory_space=pltpu.SMEM)],
        out_specs=(vmem,) * 4,
        scratch_shapes=[
            pltpu.VMEM((slots, features), BF16),
            pltpu.VMEM((1, features), F32),
            pltpu.VMEM((features, columns), BF16),
            pltpu.VMEM((features, columns), BF16),
            pltpu.VMEM((2 * rank, features), BF16),
            pltpu.VMEM((rank, columns), BF16),
            pltpu.VMEM((rank, columns), BF16),
            pltpu.VMEM((parts, rows, columns), BF16),
            pltpu.VMEM((parts, rows, columns), BF16),
            pltpu.VMEM((2 * rows, columns), BF16),
            pltpu.VMEM((2 * rows, columns), BF16),
            pltpu.VMEM((parts, rows, 2 * columns), BF16),
            pltpu.VMEM((chips, rows, 2 * columns), BF16),
            pltpu.VMEM((chips - 1, rows, 2 * columns), BF16),
            pltpu.VMEM((chips - 1, rows, 2 * columns), BF16),
            pltpu.VMEM((parts, 2 * rank, rows), F32),
            pltpu.VMEM((parts, rows, 2 * rank), BF16),
            pltpu.VMEM((parts, parts, rows), F32),
            pltpu.VMEM((2 * rank, rank), F32),
            pltpu.VMEM((parts, flat_rows, LANES), BF16),
            pltpu.VMEM((docs, flat_rows, LANES), BF16),
            dma((7,)),
            dma((parts,)),
            dma((2,)),
            dma((2,)),
            dma((2,)),
            dma((chips - 1, 2)),
            dma((chips - 1, 2)),
            dma((chips - 1, 2)),
            dma((chips - 1, 2)),
            dma((chips,)),
            dma((chips,)),
            dma((chips - 1, PIECES)),
            dma((chips - 1, PIECES)),
            dma((parts - 1,)),
            dma((parts - 1,)),
            dma((parts - 1,)),
            dma((parts - 1,)),
            dma((docs - 1,)),
            dma((docs - 1,)),
            dma((2 * chips - 1,)),
            dma((2 * chips - 1,)),
        ],
        compiler_params=pltpu.CompilerParams(
            collective_id=0, has_side_effects=True, vmem_limit_bytes=58 * 2**20
        ),
    )(
        residual,
        norm_gain.reshape(1, -1),
        key_weight,
        value_weight,
        key_grad,
        value_grad,
        key_left.T,
        value_left.T,
        key_right.T,
        value_right.T,
        queries,
        doc_lengths,
    )
    return pl.pallas_call(
        finish,
        out_shape=(
            jax.ShapeDtypeStruct((rows, columns), BF16),
            jax.ShapeDtypeStruct((rows, columns), BF16),
            jax.ShapeDtypeStruct((slots, features), BF16),
            jax.ShapeDtypeStruct((docs, queries.shape[0]), F32),
        ),
        in_specs=[vmem] * 4,
        out_specs=(hbm, hbm, hbm, vmem),
        scratch_shapes=[dma((SPLIT + 2,))],
        compiler_params=pltpu.CompilerParams(vmem_limit_bytes=2 * 2**20),
    )(key_out, value_out, hidden_grad, shares)


def solution(mesh):
    in_specs = (
        P(("groups", "dp"), "tensor"),
        P("tensor"),
        P("tensor", None),
        P("tensor", None),
        P(("groups", "dp", "tensor"), None),
        P(("groups", "dp", "tensor"), None),
        P("tensor", None),
        P("tensor", None),
        P(),
        P(),
        P(("dp", "tensor"), None),
        P(("groups", "dp")),
    )
    out_specs = (
        P(("groups", "dp", "tensor"), None),
        P(("groups", "dp", "tensor"), None),
        P(("groups", "dp"), "tensor"),
        P("groups", ("dp", "tensor")),
    )
    return jax.shard_map(body, mesh=mesh, in_specs=in_specs, out_specs=out_specs, check_vma=False)
```

```python
import functools

import jax
import jax.numpy as jnp
from jax import lax
from jax.experimental import pallas as pl
from jax.experimental.pallas import tpu as pltpu
from jax.sharding import PartitionSpec as P

F32, BF16 = jnp.float32, jnp.bfloat16
LANES = 128
PIECES = 4
SPLIT = 8


def kernel(
    parts,
    docs,
    residual,
    gain,
    key_weight,
    value_weight,
    key_grad,
    value_grad,
    key_left,
    value_left,
    key_right,
    value_right,
    queries,
    length,
    key_out,
    value_out,
    hidden_out,
    score_out,
    res_v,
    gain_v,
    kw_v,
    vw_v,
    left_w,
    kr_v,
    vr_v,
    got_k,
    got_v,
    mask_k,
    mask_v,
    partial,
    sib_in,
    x_out,
    x_in,
    left_t,
    right_g,
    squares,
    gram_rows,
    gram_in,
    flat_in,
    load_sem,
    res_sem,
    own_sem,
    ag_sib_s,
    ag_sib_r,
    ag_x_s,
    ag_x_r,
    ag_f_s,
    ag_f_r,
    rs_sib_s,
    rs_sib_r,
    rs_x_s,
    rs_x_r,
    sq_s,
    sq_r,
    gr_s,
    gr_r,
    fl_s,
    fl_r,
    rt_s,
    rt_r,
):
    chips = parts // 2
    slots, features = res_v.shape
    rows = slots // parts
    columns = kw_v.shape[1]
    rank = kr_v.shape[0]
    me = lax.axis_index("tensor")
    doc = lax.axis_index("dp")
    chip, core = me // 2, lax.rem(me, 2)
    sibling = chip * 2 + 1 - core

    def send(src, dst, s_sem, r_sem, target):
        return pltpu.make_async_remote_copy(
            src_ref=src,
            dst_ref=dst,
            send_sem=s_sem,
            recv_sem=r_sem,
            device_id=target,
            device_id_type=pl.DeviceIdType.MESH,
        )

    def chip_at(step):
        return lax.rem(chip + step + chips, chips)

    def block_of(order):
        step = lax.rem(order // 2 + 1, chips)
        other = lax.rem(order, 2)
        return chip_at(step) * 2 + jnp.where(other == 0, 1 - core, core)

    contract = (((1,), (1,)), ((), ()))

    loads = [
        pltpu.make_async_copy(src, dst, load_sem.at[i])
        for i, (src, dst) in enumerate(
            (
                (gain, gain_v),
                (key_weight, kw_v),
                (value_weight, vw_v),
                (key_left, left_w.at[:rank]),
                (value_left, left_w.at[rank:]),
                (key_right, kr_v),
                (value_right, vr_v),
            )
        )
    ]

    def res_copy(order):
        at = pl.ds(pl.multiple_of(block_of(order) * rows, rows), rows)
        return pltpu.make_async_copy(residual.at[at], res_v.at[at], res_sem.at[order])

    own_copies = [
        pltpu.make_async_copy(key_grad, got_k.at[me], own_sem.at[0]),
        pltpu.make_async_copy(value_grad, got_v.at[me], own_sem.at[1]),
    ]

    barrier = pltpu.get_barrier_semaphore()
    for step in range(1, parts):
        pl.semaphore_signal(
            barrier, inc=1, device_id={"tensor": lax.rem(me + step, parts)},
            device_id_type=pl.DeviceIdType.MESH,
        )

    def greet(step, carry):
        pl.semaphore_signal(
            barrier, inc=1, device_id={"dp": lax.rem(doc + step, docs)},
            device_id_type=pl.DeviceIdType.MESH,
        )
        return carry

    lax.fori_loop(1, docs, greet, 0)
    for order in range(parts):
        res_copy(order).start()
    for copy in own_copies + loads[5:] + loads[:5]:
        copy.start()

    pl.semaphore_wait(barrier, parts - 1 + docs - 1)

    grads = ((key_grad, got_k), (value_grad, got_v))
    ag_x = [
        [
            send(src, got.at[me], ag_x_s.at[step - 1, i], ag_x_r.at[step - 1, i],
                 {"tensor": chip_at(step) * 2 + core})
            for i, (src, got) in enumerate(grads)
        ]
        for step in range(1, chips)
    ]
    ag_sib = [
        send(src, got.at[me], ag_sib_s.at[i], ag_sib_r.at[i], {"tensor": sibling})
        for i, (src, got) in enumerate(grads)
    ]
    sq = [
        send(squares.at[me], squares.at[me], sq_s.at[step - 1], sq_r.at[step - 1],
             {"tensor": lax.rem(me + step, parts)})
        for step in range(1, parts)
    ]
    for pair in ag_x:
        pair[0].start()

    for copy in own_copies + loads[5:]:
        copy.wait()

    def masked(block, got):
        place = block * rows + lax.broadcasted_iota(jnp.int32, (rows, columns), 0)
        return got[block] * (place < length[0]).astype(F32).astype(BF16)

    for i, (got, right) in enumerate(((got_k, kr_v), (got_v, vr_v))):
        right_g[me, :, i * rank : (i + 1) * rank] = lax.dot_general(
            masked(me, got), right[...], contract, preferred_element_type=F32
        ).astype(BF16)
    def right_send(block, at, target):
        return send(right_g.at[block], right_g.at[block], rt_s.at[at], rt_r.at[at],
                    {"tensor": target})

    rt_x = [
        right_send(me, step - 1, chip_at(step) * 2 + core) for step in range(1, chips)
    ]
    rt_sib = right_send(me, chips - 1, sibling)
    for copy in rt_x + [rt_sib]:
        copy.start()

    def square(order, carry):
        res_copy(order).wait()
        block = block_of(order)
        wide = res_v[pl.ds(pl.multiple_of(block * rows, rows), rows), :].astype(F32)
        squared = wide * wide
        lane_sum = squared[:, :LANES]
        for i in range(1, features // LANES):
            lane_sum = lane_sum + squared[:, i * LANES : (i + 1) * LANES]
        squares[me, pl.ds(block, 1), :] = jnp.sum(lane_sum.T, axis=0, keepdims=True)
        return carry

    lax.fori_loop(0, parts, square, 0)
    for copy in sq:
        copy.start()
    for pair in ag_x:
        pair[1].start()
    for copy in ag_sib:
        copy.start()

    for copy in loads[:5]:
        copy.wait()

    def rs_sib(at):
        return send(partial.at[2 * at], sib_in.at[at], rs_sib_s.at[at], rs_sib_r.at[at],
                    {"tensor": sibling})

    def forward(order, carry):
        block = block_of(order)
        wide = res_v[pl.ds(pl.multiple_of(block * rows, rows), rows), :].astype(F32)
        scaled = (wide * gain_v[...]).astype(BF16)
        partial[order, :, :columns] = jnp.dot(
            scaled, kw_v[...], preferred_element_type=F32
        ).astype(BF16)
        partial[order, :, columns:] = jnp.dot(
            scaled, vw_v[...], preferred_element_type=F32
        ).astype(BF16)
        left_t[block] = lax.dot_general(
            left_w[...], scaled, contract, preferred_element_type=F32
        )

        @pl.when(lax.rem(order, 2) == 0)
        def _():
            rs_sib(order // 2).start()

        return carry

    lax.fori_loop(0, parts, forward, 0)

    rt_pass = []
    for step in range(1, chips):
        rt_x[step - 1].wait_recv()
        origin = chip_at(-step) * 2 + core
        rt_pass.append(right_send(origin, chips - 1 + step, sibling))
        rt_pass[-1].start()

    size = rows // PIECES
    pieces = [slice(i * size, (i + 1) * size) for i in range(PIECES)]
    rs_x = []
    for step in range(1, chips):
        at = step - 1
        rs_sib(at).wait_recv()
        x_out[at] = (
            partial[2 * at + 1].astype(F32) + sib_in[at].astype(F32)
        ).astype(BF16)
        rs_x.append(
            [
                send(x_out.at[at, here], x_in.at[at, here], rs_x_s.at[at, i], rs_x_r.at[at, i],
                     {"tensor": chip_at(step) * 2 + core})
                for i, here in enumerate(pieces)
            ]
        )

    def inverse_of(block):
        total = squares[0, pl.ds(block, 1), :]
        for i in range(1, parts):
            total = total + squares[i, pl.ds(block, 1), :]
        return lax.rsqrt(total / (features * parts) + 1e-05)

    span = 2 * rows
    tile = min(features, 512)

    def mask_chip(at):
        for half in range(2):
            block = at * 2 + half
            mask_k[half * rows : (half + 1) * rows, :] = masked(block, got_k)
            mask_v[half * rows : (half + 1) * rows, :] = masked(block, got_v)

    def gram_share():
        def add(block, total):
            left = left_t[block] * inverse_of(block)
            right = right_g[block].astype(F32)
            return tuple(
                was
                + jnp.dot(
                    left[i * rank : (i + 1) * rank],
                    right[:, i * rank : (i + 1) * rank],
                    precision=lax.Precision.HIGHEST,
                    preferred_element_type=F32,
                )
                for i, was in enumerate(total)
            )

        zero = jnp.zeros((rank, rank), F32)
        for i, share in enumerate(lax.fori_loop(0, parts, add, (zero, zero))):
            gram_rows[i * rank : (i + 1) * rank, :] = share

    def back(at):
        to = pl.ds(pl.multiple_of(at * span, span), span)

        def one(i, carry):
            here = pl.ds(pl.multiple_of(i * tile, tile), tile)
            total = lax.dot_general(
                mask_k[...], kw_v[here, :], contract, preferred_element_type=F32
            ) + lax.dot_general(
                mask_v[...], vw_v[here, :], contract, preferred_element_type=F32
            )
            hidden_out[to, here] = total.astype(BF16)
            return carry

        lax.fori_loop(0, features // tile, one, 0)

    for copy in sq + [rt_sib] + rt_pass:
        copy.wait_recv()
    gram_share()
    half = gram_rows.shape[0] // 2
    gram_in[me] = jnp.concatenate(
        [gram_rows[pl.ds(0, half, stride=2), :], gram_rows[pl.ds(1, half, stride=2), :]],
        axis=1,
    ).astype(BF16)
    gr = [
        send(gram_in.at[me], gram_in.at[me], gr_s.at[to - 1], gr_r.at[to - 1],
             {"tensor": lax.rem(me + to, parts)})
        for to in range(1, parts)
    ]
    for copy in gr:
        copy.start()

    for i in range(PIECES):
        for group in rs_x:
            group[i].start()

    for copy in ag_sib:
        copy.wait_recv()
    mask_chip(chip)
    back(chip)

    passed = []
    for step in range(1, chips):
        origin = chip_at(-step) * 2 + core
        for i, (_, got) in enumerate(grads):
            ag_x[step - 1][i].wait_recv()
            copy = send(got.at[origin], got.at[origin], ag_f_s.at[step - 1, i],
                        ag_f_r.at[step - 1, i], {"tensor": sibling})
            copy.start()
            passed.append(copy)

    for copy in gr:
        copy.wait_recv()
    gram = gram_in[0].astype(F32)
    for i in range(1, parts):
        gram = gram + gram_in[i].astype(F32)
    flat_in[doc] = (gram / slots).astype(BF16)

    def flat_copy(step):
        return send(flat_in.at[doc], flat_in.at[doc], fl_s.at[step - 1], fl_r.at[step - 1],
                    {"dp": lax.rem(doc + step, docs)})

    def flat_start(step, carry):
        flat_copy(step).start()
        return carry

    def flat_wait(step, carry):
        flat_copy(step).wait()
        return carry

    lax.fori_loop(1, docs, flat_start, 0)

    for step in range(1, chips):
        for i in range(2):
            passed[2 * (step - 1) + i].wait_recv()
        mask_chip(chip_at(-step))
        back(chip_at(-step))

    last = chips - 1
    rs_sib(last).wait_recv()
    inverse = jnp.broadcast_to(inverse_of(me), (LANES, rows)).T

    lax.fori_loop(1, docs, flat_wait, 0)

    def score(i, carry):
        flat = flat_in[i].astype(F32)
        total = jnp.zeros((queries.shape[0], LANES), F32)
        for j in range(flat.shape[0]):
            total = total + queries[:, j * LANES : (j + 1) * LANES].astype(F32) * flat[j : j + 1]
        score_out[i] = total
        return carry

    lax.fori_loop(0, docs, score, 0)

    for at, piece in enumerate(pieces):
        for group in rs_x:
            group[at].wait_recv()
        own = partial[2 * last + 1, piece].astype(F32) + sib_in[last, piece].astype(F32)
        for i in range(chips - 1):
            own = own + x_in[i, piece].astype(F32)
        scale = inverse[piece]
        for i in range(columns // LANES):
            here = slice(i * LANES, (i + 1) * LANES)
            there = slice(columns + i * LANES, columns + (i + 1) * LANES)
            key_out[piece, here] = (own[:, here] * scale).astype(BF16)
            value_out[piece, here] = (own[:, there] * scale).astype(BF16)

    for copy in rt_x + [rt_sib] + rt_pass + ag_sib + [copy for pair in ag_x for copy in pair] + passed + sq + gr + [copy for group in rs_x for copy in group]:
        copy.wait_send()
    for i in range(chips):
        rs_sib(i).wait_send()


def finish(key_in, value_in, hidden_in, shares, key_out, value_out, hidden_out, scores, sem):
    size = hidden_in.shape[0] // SPLIT
    views = [slice(i * size, (i + 1) * size) for i in range(SPLIT)]
    pairs = [(hidden_in.at[here], hidden_out.at[here]) for here in views]
    pairs += [(key_in, key_out), (value_in, value_out)]
    copies = [
        pltpu.make_async_copy(src, dst, sem.at[i]) for i, (src, dst) in enumerate(pairs)
    ]
    for copy in copies:
        copy.start()
    scores[...] = jnp.sum(shares[...], axis=2)
    for copy in copies:
        copy.wait()


def body(
    residual,
    norm_gain,
    key_weight,
    value_weight,
    key_grad,
    value_grad,
    key_left,
    value_left,
    key_right,
    value_right,
    queries,
    doc_lengths,
):
    parts, docs = lax.axis_size("tensor"), lax.axis_size("dp")
    chips = parts // 2
    slots, features = residual.shape
    rows = slots // parts
    columns, rank = key_weight.shape[1], key_left.shape[1]
    hbm = pl.BlockSpec(memory_space=pl.ANY)
    vmem = pl.BlockSpec(memory_space=pltpu.VMEM)
    dma = pltpu.SemaphoreType.DMA
    flat_rows = 2 * rank * rank // LANES
    key_out, value_out, hidden_grad, shares = pl.pallas_call(
        functools.partial(kernel, parts, docs),
        out_shape=(
            pltpu.VMEM((rows, columns), BF16),
            pltpu.VMEM((rows, columns), BF16),
            pltpu.VMEM((slots, features), BF16),
            pltpu.VMEM((docs, queries.shape[0], LANES), F32),
        ),
        in_specs=[hbm] * 10 + [vmem, pl.BlockSpec(memory_space=pltpu.SMEM)],
        out_specs=(vmem,) * 4,
        scratch_shapes=[
            pltpu.VMEM((slots, features), BF16),
            pltpu.VMEM((1, features), F32),
            pltpu.VMEM((features, columns), BF16),
            pltpu.VMEM((features, columns), BF16),
            pltpu.VMEM((2 * rank, features), BF16),
            pltpu.VMEM((rank, columns), BF16),
            pltpu.VMEM((rank, columns), BF16),
            pltpu.VMEM((parts, rows, columns), BF16),
            pltpu.VMEM((parts, rows, columns), BF16),
            pltpu.VMEM((2 * rows, columns), BF16),
            pltpu.VMEM((2 * rows, columns), BF16),
            pltpu.VMEM((parts, rows, 2 * columns), BF16),
            pltpu.VMEM((chips, rows, 2 * columns), BF16),
            pltpu.VMEM((chips - 1, rows, 2 * columns), BF16),
            pltpu.VMEM((chips - 1, rows, 2 * columns), BF16),
            pltpu.VMEM((parts, 2 * rank, rows), F32),
            pltpu.VMEM((parts, rows, 2 * rank), BF16),
            pltpu.VMEM((parts, parts, rows), F32),
            pltpu.VMEM((2 * rank, rank), F32),
            pltpu.VMEM((parts, flat_rows, LANES), BF16),
            pltpu.VMEM((docs, flat_rows, LANES), BF16),
            dma((7,)),
            dma((parts,)),
            dma((2,)),
            dma((2,)),
            dma((2,)),
            dma((chips - 1, 2)),
            dma((chips - 1, 2)),
            dma((chips - 1, 2)),
            dma((chips - 1, 2)),
            dma((chips,)),
            dma((chips,)),
            dma((chips - 1, PIECES)),
            dma((chips - 1, PIECES)),
            dma((parts - 1,)),
            dma((parts - 1,)),
            dma((parts - 1,)),
            dma((parts - 1,)),
            dma((docs - 1,)),
            dma((docs - 1,)),
            dma((2 * chips - 1,)),
            dma((2 * chips - 1,)),
        ],
        compiler_params=pltpu.CompilerParams(
            collective_id=0, has_side_effects=True, vmem_limit_bytes=58 * 2**20
        ),
    )(
        residual,
        norm_gain.reshape(1, -1),
        key_weight,
        value_weight,
        key_grad,
        value_grad,
        key_left.T,
        value_left.T,
        key_right.T,
        value_right.T,
        queries,
        doc_lengths,
    )
    return pl.pallas_call(
        finish,
        out_shape=(
            jax.ShapeDtypeStruct((rows, columns), BF16),
            jax.ShapeDtypeStruct((rows, columns), BF16),
            jax.ShapeDtypeStruct((slots, features), BF16),
            jax.ShapeDtypeStruct((docs, queries.shape[0]), F32),
        ),
        in_specs=[vmem] * 4,
        out_specs=(hbm, hbm, hbm, vmem),
        scratch_shapes=[dma((SPLIT + 2,))],
        compiler_params=pltpu.CompilerParams(vmem_limit_bytes=2 * 2**20),
    )(key_out, value_out, hidden_grad, shares)


def solution(mesh):
    in_specs = (
        P(("groups", "dp"), "tensor"),
        P("tensor"),
        P("tensor", None),
        P("tensor", None),
        P(("groups", "dp", "tensor"), None),
        P(("groups", "dp", "tensor"), None),
        P("tensor", None),
        P("tensor", None),
        P(),
        P(),
        P(("dp", "tensor"), None),
        P(("groups", "dp")),
    )
    out_specs = (
        P(("groups", "dp", "tensor"), None),
        P(("groups", "dp", "tensor"), None),
        P(("groups", "dp"), "tensor"),
        P("groups", ("dp", "tensor")),
    )
    return jax.shard_map(body, mesh=mesh, in_specs=in_specs, out_specs=out_specs, check_vma=False)
```
